32 devices in a mesh: dp: 4 (over z), ctx: 8 (over y, x, core).
Axes of the slice: x: 2, y: 2, z: 4, core: 2. Of those that a mesh axis runs over, the one named last changes fastest.
Arguments:
- tokens: bfloat16 [4, 262144, 128], P('dp', 'ctx'), may hold values from -6 to 6
- cotangent: bfloat16 [4, 262144, 128], P('dp', 'ctx'), may hold values from -6 to 6
- w_gate_value: bfloat16 [128, 256], replicated, may hold values from -0.5 to 0.5
- w_first: bfloat16 [512, 512], replicated, may hold values from -0.25 to 0.25
- w_second: bfloat16 [512, 512], replicated, may hold values from -0.25 to 0.25
- w_up: bfloat16 [128, 256], replicated, may hold values from -0.5 to 0.5
- w_down: bfloat16 [256, 128], replicated, may hold values from -0.375 to 0.375
Outputs:
- output: bfloat16 [4, 262144, 128], P('dp', 'ctx')
- grad_tokens: bfloat16 [4, 262144, 128], P('dp', 'ctx')
- grad_gate_value: float32 [128, 256], replicated
- grad_first: float32 [512, 512], replicated
- grad_second: float32 [512, 512], replicated
- grad_up: float32 [128, 256], replicated
- grad_down: float32 [256, 128], replicated
The draws below stay inside these ranges and needn't reach their ends.
All inputs are finite; a program needn't handle non-finite values.
Results may differ from the reference program's by a relative error of at most 0.014.
Values may be sent and summed in bfloat16 or wider, within the bound.
A program may use at most 256 MiB of HBM per device.

```python
import jax
import jax.numpy as jnp
from jax import lax

NB = 512
BS = 512
CH = 128
FF = 256
SEQLEN = 262144
SEQS = 4


def level_of(key, shape, cuts, low, top_value):
    factor_of, own = 1.0, jax.random.fold_in(key, 6)
    for axis_at, shards_of in cuts:
        steps = jnp.exp(jax.random.uniform(jax.random.fold_in(own, axis_at), (shards_of,), jnp.float32, low / len(cuts), top_value / len(cuts)))
        factor_of = factor_of * jnp.repeat(steps, shape[axis_at] // shards_of).reshape([-1 if axis == axis_at else 1 for axis in range(len(shape))])
    return factor_of


def centred(stream_key, extent, deviation, reach, pieces=(), dtype=jnp.bfloat16):
    drawn = jax.random.normal(stream_key, extent, jnp.float32) * deviation
    if len(pieces) > 0:
        drawn = level_of(stream_key, extent, pieces, -0.22, 0.18) * drawn
    return jnp.clip(drawn, min=-reach, max=reach).astype(dtype)


def setup_inputs(seed: int = 0) -> dict:
    splits = jax.random.split(jax.random.key(seed), 8)
    tokens = centred(splits[0], (SEQS, SEQLEN, CH), 1.0, 6.0, ((0, 4), (1, 8)))
    cotangent = centred(splits[1], (SEQS, SEQLEN, CH), 1.0, 6.0, ((0, 4), (1, 8)))
    w_gate_value = centred(splits[2], (CH, 2 * CH), CH ** -0.5, 0.5)
    w_first = centred(splits[3], (BS, BS), BS ** -0.5, 0.25)
    w_second = centred(splits[4], (NB, NB), NB ** -0.5, 0.25)
    w_up = centred(splits[5], (CH, FF), CH ** -0.5, 0.5)
    w_down = centred(splits[6], (FF, CH), FF ** -0.5, 0.375)
    return dict(tokens=tokens, cotangent=cotangent, w_gate_value=w_gate_value, w_first=w_first, w_second=w_second, w_up=w_up, w_down=w_down)


def silu_slope(pre):
    sigma = jax.nn.sigmoid(pre)
    return sigma * (1.0 + pre * (1.0 - sigma))


def one_sequence(seq_in, seq_cot, w_gate_value, w_first, w_second, w_up, w_down):
    f32 = jnp.float32
    bf16 = jnp.bfloat16
    projected = jnp.dot(seq_in, w_gate_value, preferred_element_type=f32)
    gate = jax.nn.sigmoid(projected[:, :CH])
    values = projected[:, CH:].astype(bf16)
    value_blocks = values.reshape(NB, BS, CH)
    first = jnp.einsum("ijc,jk->ikc", value_blocks.astype(f32), w_first.astype(f32)).astype(bf16)
    mixed = jnp.einsum("ikc,im->mkc", first.astype(f32), w_second.astype(f32)).astype(bf16).reshape(SEQLEN, CH)
    hidden = (seq_in.astype(f32) + gate * mixed.astype(f32)).astype(bf16)
    pre = jnp.dot(hidden, w_up, preferred_element_type=f32)
    activated = jax.nn.silu(pre).astype(bf16)
    output = (hidden.astype(f32) + jnp.dot(activated, w_down, preferred_element_type=f32)).astype(bf16)
    grad_down = jnp.dot(activated.T, seq_cot, preferred_element_type=f32)
    d_act = (jnp.dot(seq_cot, w_down.T, preferred_element_type=f32) * silu_slope(pre)).astype(bf16)
    grad_up = jnp.dot(hidden.T, d_act, preferred_element_type=f32)
    d_hidden = (seq_cot.astype(f32) + jnp.dot(d_act, w_up.T, preferred_element_type=f32)).astype(bf16)
    d_mixed = (d_hidden.astype(f32) * gate).astype(bf16).reshape(NB, BS, CH)
    d_gate = d_hidden.astype(f32) * mixed.astype(f32) * gate * (1.0 - gate)
    d_first = jnp.einsum("mkc,im->ikc", d_mixed.astype(f32), w_second.astype(f32)).astype(bf16)
    grad_second = jnp.einsum("ikc,mkc->im", first.astype(f32), d_mixed.astype(f32))
    d_values = jnp.einsum("ikc,jk->ijc", d_first.astype(f32), w_first.astype(f32)).reshape(SEQLEN, CH)
    grad_first = jnp.einsum("ijc,ikc->jk", value_blocks.astype(f32), d_first.astype(f32))
    d_projected = jnp.concatenate([d_gate, d_values], axis=1).astype(bf16)
    grad_gate_value = jnp.dot(seq_in.T, d_projected, preferred_element_type=f32)
    grad_tokens = (d_hidden.astype(f32) + jnp.dot(d_projected, w_gate_value.T, preferred_element_type=f32)).astype(bf16)
    return output, grad_tokens, (grad_gate_value, grad_first, grad_second, grad_up, grad_down)


def reference(tokens, cotangent, w_gate_value, w_first, w_second, w_up, w_down):
    f32 = jnp.float32
    start = (jnp.zeros((CH, 2 * CH), f32), jnp.zeros((BS, BS), f32), jnp.zeros((NB, NB), f32),
             jnp.zeros((CH, FF), f32), jnp.zeros((FF, CH), f32))

    def step_fn(totals, pair):
        output, grad_tokens, grads = one_sequence(pair[0], pair[1], w_gate_value, w_first, w_second, w_up, w_down)
        return jax.tree.map(lambda left, right: left + right, totals, grads), (output, grad_tokens)

    totals, outs = lax.scan(step_fn, start, (tokens, cotangent))
    scale = float(SEQS * SEQLEN) ** -0.5
    return (outs[0], outs[1], totals[0] * scale, totals[1] * scale, totals[2] * scale,
            totals[3] * scale, totals[4] * scale)
```

```python
import functools

import jax
import jax.numpy as jnp
from jax import lax
from jax.experimental import pallas as pl
from jax.experimental.pallas import tpu as pltpu
from jax.sharding import PartitionSpec as P

F32 = jnp.float32
BF16 = jnp.bfloat16
TILE = 16
VMEM_LIMIT = 56 * 1024 * 1024


def sig(v):
    return 0.5 * jnp.tanh(0.5 * v) + 0.5


def dot(a, b):
    return jnp.dot(a, b, preferred_element_type=F32)


def dot_rows(a, b):
    return lax.dot_general(a, b, (((0,), (0,)), ((), ())), preferred_element_type=F32)


def dot_lanes(a, b):
    return lax.dot_general(a, b, (((1,), (1,)), ((), ())), preferred_element_type=F32)


def lanes(ref, count):
    return jnp.concatenate([ref[b] for b in range(count)], axis=1)


def params():
    return pltpu.CompilerParams(vmem_limit_bytes=VMEM_LIMIT)


def cost(flops, nbytes, trans=0):
    return pl.CostEstimate(flops=int(flops), bytes_accessed=int(nbytes), transcendentals=int(trans))


def whole(array):
    zeros = (0,) * array.ndim
    return pl.BlockSpec(array.shape, lambda *_: zeros)


def first_kernel(from_tokens, *refs):
    if from_tokens:
        src, wv, w1t, val, *outs = refs
        rows = src.shape[0] * src.shape[1]
        val[...] = dot(src[...].reshape(rows, src.shape[2]), wv[...]).astype(BF16).reshape(val.shape)
    else:
        val, w1t, *outs = refs
    width = val.shape[2]
    vals = lanes(val, TILE)
    per = outs[0].shape[0]
    for at, out in enumerate(outs):
        res = dot(w1t[at * per : (at + 1) * per, :], vals)
        parts = jnp.stack([res[:, b * width : (b + 1) * width] for b in range(TILE)], 0)
        out[...] = jnp.swapaxes(parts, 0, 1).astype(BF16)


def first_call(src, wv, w1t, per):
    blocks, steps, width = src.shape
    outs = w1t.shape[0] // per
    tile = pl.BlockSpec((TILE, steps, width), lambda t: (t, 0, 0))
    sent = pl.BlockSpec((per, TILE, width), lambda t: (0, t, 0))
    sent_shape = jax.ShapeDtypeStruct((per, blocks, width), BF16)
    flops = 2 * blocks * steps * width * w1t.shape[0]
    if wv is not None:
        return pl.pallas_call(
            functools.partial(first_kernel, True),
            grid=(blocks // TILE,),
            in_specs=[tile, whole(wv), whole(w1t)],
            out_specs=[tile] + [sent] * outs,
            out_shape=[jax.ShapeDtypeStruct(src.shape, BF16)] + [sent_shape] * outs,
            compiler_params=params(),
            cost_estimate=cost(flops + 2 * src.size * width, 4 * src.size + 2 * per * blocks * width),
            name="values_first",
        )(src, wv, w1t)
    return pl.pallas_call(
        functools.partial(first_kernel, False),
        grid=(blocks // TILE,),
        in_specs=[tile, whole(w1t)],
        out_specs=[sent] * outs,
        out_shape=[sent_shape] * outs,
        compiler_params=params(),
        cost_estimate=cost(flops, 2 * src.size + 2 * outs * per * blocks * width),
        name="first_rest",
    )(src, w1t)


def gather_positions(ref, count, order, width):
    return jnp.concatenate([ref[:, q].reshape(order, width) for q in range(count)], axis=1)


def spread_positions(ref, res, count, width):
    n, _, rows, _ = ref.shape
    for q in range(count):
        ref[:, q] = res[:, q * width : (q + 1) * width].astype(BF16).reshape(n, rows, width)


def mix_kernel(x, w, out):
    n, count, rows, width = x.shape
    spread_positions(out, dot(w[...], gather_positions(x, count, n * rows, width)), count, width)


def mix_back_kernel(x, d, w, out, grad):
    n, count, rows, width = x.shape

    @pl.when(pl.program_id(0) == 0)
    def _():
        grad[...] = jnp.zeros_like(grad)

    dm = gather_positions(d, count, n * rows, width)
    spread_positions(out, dot(w[...], dm), count, width)
    grad[...] += dot_lanes(gather_positions(x, count, n * rows, width), dm)


def mix_call(x, w):
    n, per, rows, width = x.shape
    count = min(4, per)
    spec = pl.BlockSpec((n, count, rows, width), lambda t: (0, t, 0, 0))
    return pl.pallas_call(
        mix_kernel,
        grid=(per // count,),
        in_specs=[spec, whole(w)],
        out_specs=spec,
        out_shape=jax.ShapeDtypeStruct(x.shape, BF16),
        compiler_params=params(),
        cost_estimate=cost(2 * x.size * w.shape[0], 4 * x.size),
        name="mix",
    )(x, w)


def mix_back_call(x, d, w):
    n, per, rows, width = x.shape
    count = min(4, per)
    spec = pl.BlockSpec((n, count, rows, width), lambda t: (0, t, 0, 0))
    return pl.pallas_call(
        mix_back_kernel,
        grid=(per // count,),
        in_specs=[spec, spec, whole(w)],
        out_specs=[spec, whole(w)],
        out_shape=[jax.ShapeDtypeStruct(x.shape, BF16), jax.ShapeDtypeStruct(w.shape, F32)],
        compiler_params=params(),
        cost_estimate=cost(4 * x.size * w.shape[0], 6 * x.size),
        name="mix_back",
    )(x, d, w)


def mlp_kernel(tok, cot, mix, wg, wgt, wu, wut, wd, wdt, *rest):
    out, part, dmix, gdown, gup, ggate, mixed, dback = rest[-8:]
    width = tok.shape[2]
    steps = tok.shape[1]
    sub = 4

    @pl.when(pl.program_id(0) == 0)
    def _():
        gdown[...] = jnp.zeros_like(gdown)
        gup[...] = jnp.zeros_like(gup)
        ggate[...] = jnp.zeros_like(ggate)

    mixed[...] = jnp.swapaxes(mix[...].astype(F32), 0, 1)

    @pl.loop(0, TILE // sub)
    def _(s):
        at = pl.ds(s * sub, sub)
        flat = (sub * steps, width)
        back = (sub, steps, width)
        t = tok[at].reshape(flat)
        ct = cot[at].reshape(flat)
        m = mixed[at].reshape(flat)
        gate = sig(dot(t, wg[...]))
        hidden = (t.astype(F32) + gate * m).astype(BF16)
        pre = dot(hidden, wu[...])
        sg = sig(pre)
        act = (pre * sg).astype(BF16)
        out[at] = (hidden.astype(F32) + dot(act, wd[...])).astype(BF16).reshape(back)
        dact = (dot(ct, wdt[...]) * (sg * (1.0 + pre * (1.0 - sg)))).astype(BF16)
        gdown[...] += dot_rows(act, ct)
        gup[...] += dot_rows(hidden, dact)
        dh = (ct.astype(F32) + dot(dact, wut[...])).astype(BF16).astype(F32)
        dm = dh * gate
        dback[at] = dm.reshape(back)
        dgate = (dm * m * (1.0 - gate)).astype(BF16)
        part[at] = (dh + dot(dgate, wgt[...])).astype(BF16).reshape(back)
        ggate[...] += dot_rows(t, dgate)

    dmix[...] = jnp.swapaxes(dback[...], 0, 1).astype(BF16)


def mlp_call(chunk, tokens, cot, mix, weights, carried):
    blocks, steps, width = tokens.shape
    per = mix.shape[0]
    wg, wgt, wu, wut, wd, wdt = weights
    tile = pl.BlockSpec((TILE, per, width), lambda t: (t, chunk, 0))
    mid = pl.BlockSpec((per, TILE, width), lambda t: (0, t, 0))
    held = [pl.BlockSpec(memory_space=pl.ANY)] * len(carried)
    grads = [wd, wu, wg]
    rows = blocks * per
    full = jax.ShapeDtypeStruct(tokens.shape, BF16)
    return pl.pallas_call(
        mlp_kernel,
        grid=(blocks // TILE,),
        in_specs=[tile, tile, mid] + [whole(w) for w in weights] + held,
        out_specs=[tile, tile, mid] + [whole(g) for g in grads],
        out_shape=[full, full, jax.ShapeDtypeStruct(mix.shape, BF16)]
        + [jax.ShapeDtypeStruct(g.shape, F32) for g in grads],
        scratch_shapes=[pltpu.VMEM((TILE, per, width), F32)] * 2,
        input_output_aliases={9 + a: a for a in range(len(carried))},
        compiler_params=params(),
        cost_estimate=cost(2 * rows * (6 * wu.size + 3 * wg.size), 12 * rows * width, rows * 3 * width),
        name="mlp",
    )(tokens, cot, mix, *weights, *carried)


def back_kernel(d, val, *rest):
    out, grad = rest[-2:]

    @pl.when(pl.program_id(0) == 0)
    def _():
        grad[...] = jnp.zeros_like(grad)

    out[...] = jnp.swapaxes(d[...].astype(F32), 0, 1).astype(BF16)
    grad[...] += dot_lanes(lanes(val, TILE), lanes(out, TILE))


def back_call(chunk, d, values, carried):
    blocks, steps, width = values.shape
    per = d.shape[0]
    held = [pl.BlockSpec(memory_space=pl.ANY)] * len(carried)
    return pl.pallas_call(
        back_kernel,
        grid=(blocks // TILE,),
        in_specs=[
            pl.BlockSpec((per, TILE, width), lambda t: (0, t, 0)),
            pl.BlockSpec((TILE, steps, width), lambda t: (t, 0, 0)),
        ]
        + held,
        out_specs=[
            pl.BlockSpec((TILE, per, width), lambda t: (t, chunk, 0)),
            pl.BlockSpec((steps, per), lambda t: (0, 0)),
        ],
        out_shape=[
            jax.ShapeDtypeStruct(values.shape, BF16),
            jax.ShapeDtypeStruct((steps, per), F32),
        ],
        input_output_aliases={2 + a: a for a in range(len(carried))},
        compiler_params=params(),
        cost_estimate=cost(2 * values.size * per, 2 * values.size + 4 * d.size),
        name="first_back",
    )(d, values, *carried)


def tokens_kernel(d, part, tok, w1, wvt, out, grad):
    width = tok.shape[2]

    @pl.when(pl.program_id(0) == 0)
    def _():
        grad[...] = jnp.zeros_like(grad)

    res = dot(w1[...], lanes(d, TILE))
    total = grad[...]
    for b in range(TILE):
        dv = res[:, b * width : (b + 1) * width].astype(BF16)
        out[b] = (part[b].astype(F32) + dot(dv, wvt[...])).astype(BF16)
        total += dot_rows(tok[b], dv)
    grad[...] = total


def tokens_call(d, part, tokens, w1, wvt):
    blocks, steps, width = tokens.shape
    tile = pl.BlockSpec((TILE, steps, width), lambda t: (t, 0, 0))
    return pl.pallas_call(
        tokens_kernel,
        grid=(blocks // TILE,),
        in_specs=[tile, tile, tile, whole(w1), whole(wvt)],
        out_specs=[tile, whole(wvt)],
        out_shape=[jax.ShapeDtypeStruct(tokens.shape, BF16), jax.ShapeDtypeStruct(wvt.shape, F32)],
        compiler_params=params(),
        cost_estimate=cost(2 * tokens.size * (steps + 2 * width), 8 * tokens.size),
        name="grad_tokens",
    )(d, part, tokens, w1, wvt)


def body(tokens, cotangent, w_gate_value, w_first, w_second, w_up, w_down):
    n = lax.axis_size("ctx")
    seq_rows, width = tokens.shape[1:]
    steps = w_first.shape[0]
    blocks = seq_rows // steps
    chunks = 4
    per = steps // chunks
    tok = tokens.reshape(blocks, steps, width)
    cot = cotangent.reshape(blocks, steps, width)
    wg, wv = w_gate_value[:, :width], w_gate_value[:, width:]
    w1t = w_first.T
    w2t = w_second.T
    weights = (wg, wg.T, w_up, w_up.T, w_down, w_down.T)

    def exchange(a):
        moved = lax.all_to_all(
            a.reshape(n, per // n, blocks, width), "ctx", split_axis=0, concat_axis=0, tiled=True
        )
        return moved

    values, lead = first_call(tok, wv, w1t[:per], per)
    firsts = [lead, *first_call(values, None, w1t[per:], per)]

    first_mid, mixed, d_mixed, d_first = {}, {}, {}, {}
    small, second, first_cols = [], [], []
    carried, carried_d = (), ()
    for at in range(chunks + 3):
        if at < chunks:
            first_mid[at] = exchange(firsts[at])
        c = at - 1
        if 0 <= c < chunks:
            mixed[c] = exchange(mix_call(first_mid[c], w2t)).reshape(per, blocks, width)
        c = at - 2
        if 0 <= c < chunks:
            out, part, dm, *grads = mlp_call(c, tok, cot, mixed[c], weights, carried)
            carried = (out, part)
            small.append(grads)
            d_mixed[c] = exchange(dm)
        c = at - 3
        if 0 <= c < chunks:
            df, g2 = mix_back_call(first_mid[c], d_mixed[c], w_second)
            second.append(g2)
            d_first[c] = exchange(df).reshape(per, blocks, width)
    for c in range(chunks):
        filled, cols = back_call(c, d_first[c], values, carried_d)
        carried_d = (filled,)
        first_cols.append(cols)
    grad_down, grad_up, grad_gate = [sum(parts) for parts in zip(*small)]
    grad_tokens, grad_value = tokens_call(carried_d[0], carried[1], tok, w_first, wv.T)

    axes = ("dp", "ctx")
    scale = float(seq_rows * n * lax.axis_size("dp")) ** (-0.5)
    grad_second = sum(second)
    grad_down, grad_up, grad_gate, grad_second = lax.psum(
        (grad_down, grad_up, grad_gate, grad_second), axes
    )
    *cols, grad_value = lax.psum((*first_cols, grad_value), axes)
    return (
        carried[0].reshape(tokens.shape),
        grad_tokens.reshape(tokens.shape),
        jnp.concatenate([grad_gate, grad_value], axis=1) * scale,
        jnp.concatenate(cols, axis=1) * scale,
        grad_second * scale,
        grad_up * scale,
        grad_down * scale,
    )


def solution(mesh):
    placed = (P("dp", "ctx", None), P("dp", "ctx", None), P(), P(), P(), P(), P())
    return jax.shard_map(
        body,
        mesh=mesh,
        in_specs=placed,
        out_specs=(P("dp", "ctx", None), P("dp", "ctx", None), P(), P(), P(), P(), P()),
        check_vma=False,
    )
```

```python
import functools

import jax
import jax.numpy as jnp
from jax import lax
from jax.experimental import pallas as pl
from jax.experimental.pallas import tpu as pltpu
from jax.sharding import PartitionSpec as P

F32 = jnp.float32
BF16 = jnp.bfloat16
TILE = 16
VMEM_LIMIT = 56 * 1024 * 1024


def sig(v):
    return 0.5 * jnp.tanh(0.5 * v) + 0.5


def dot(a, b):
    return jnp.dot(a, b, preferred_element_type=F32)


def dot_rows(a, b):
    return lax.dot_general(a, b, (((0,), (0,)), ((), ())), preferred_element_type=F32)


def dot_lanes(a, b):
    return lax.dot_general(a, b, (((1,), (1,)), ((), ())), preferred_element_type=F32)


def lanes(ref, count):
    return jnp.concatenate([ref[b] for b in range(count)], axis=1)


def params():
    return pltpu.CompilerParams(vmem_limit_bytes=VMEM_LIMIT)


def cost(flops, nbytes, trans=0):
    return pl.CostEstimate(flops=int(flops), bytes_accessed=int(nbytes), transcendentals=int(trans))


def whole(array):
    zeros = (0,) * array.ndim
    return pl.BlockSpec(array.shape, lambda *_: zeros)


def first_kernel(from_tokens, *refs):
    if from_tokens:
        src, wv, w1t, val, *outs = refs
        rows = src.shape[0] * src.shape[1]
        val[...] = dot(src[...].reshape(rows, src.shape[2]), wv[...]).astype(BF16).reshape(val.shape)
    else:
        val, w1t, *outs = refs
    width = val.shape[2]
    vals = lanes(val, TILE)
    per = outs[0].shape[0]
    for at, out in enumerate(outs):
        res = dot(w1t[at * per : (at + 1) * per, :], vals)
        parts = jnp.stack([res[:, b * width : (b + 1) * width] for b in range(TILE)], 0)
        out[...] = jnp.swapaxes(parts, 0, 1).astype(BF16)


def first_call(src, wv, w1t, per):
    blocks, steps, width = src.shape
    outs = w1t.shape[0] // per
    tile = pl.BlockSpec((TILE, steps, width), lambda t: (t, 0, 0))
    sent = pl.BlockSpec((per, TILE, width), lambda t: (0, t, 0))
    sent_shape = jax.ShapeDtypeStruct((per, blocks, width), BF16)
    flops = 2 * blocks * steps * width * w1t.shape[0]
    if wv is not None:
        return pl.pallas_call(
            functools.partial(first_kernel, True),
            grid=(blocks // TILE,),
            in_specs=[tile, whole(wv), whole(w1t)],
            out_specs=[tile] + [sent] * outs,
            out_shape=[jax.ShapeDtypeStruct(src.shape, BF16)] + [sent_shape] * outs,
            compiler_params=params(),
            cost_estimate=cost(flops + 2 * src.size * width, 4 * src.size + 2 * per * blocks * width),
            name="values_first",
        )(src, wv, w1t)
    return pl.pallas_call(
        functools.partial(first_kernel, False),
        grid=(blocks // TILE,),
        in_specs=[tile, whole(w1t)],
        out_specs=[sent] * outs,
        out_shape=[sent_shape] * outs,
        compiler_params=params(),
        cost_estimate=cost(flops, 2 * src.size + 2 * outs * per * blocks * width),
        name="first_rest",
    )(src, w1t)


def gather_positions(ref, count, order, width):
    return jnp.concatenate([ref[:, q].reshape(order, width) for q in range(count)], axis=1)


def spread_positions(ref, res, count, width):
    n, _, rows, _ = ref.shape
    for q in range(count):
        ref[:, q] = res[:, q * width : (q + 1) * width].astype(BF16).reshape(n, rows, width)


def mix_kernel(x, w, out):
    n, count, rows, width = x.shape
    spread_positions(out, dot(w[...], gather_positions(x, count, n * rows, width)), count, width)


def mix_back_kernel(x, d, w, out, grad):
    n, count, rows, width = x.shape

    @pl.when(pl.program_id(0) == 0)
    def _():
        grad[...] = jnp.zeros_like(grad)

    dm = gather_positions(d, count, n * rows, width)
    spread_positions(out, dot(w[...], dm), count, width)
    grad[...] += dot_lanes(gather_positions(x, count, n * rows, width), dm)


def mix_call(x, w):
    n, per, rows, width = x.shape
    count = min(4, per)
    spec = pl.BlockSpec((n, count, rows, width), lambda t: (0, t, 0, 0))
    return pl.pallas_call(
        mix_kernel,
        grid=(per // count,),
        in_specs=[spec, whole(w)],
        out_specs=spec,
        out_shape=jax.ShapeDtypeStruct(x.shape, BF16),
        compiler_params=params(),
        cost_estimate=cost(2 * x.size * w.shape[0], 4 * x.size),
        name="mix",
    )(x, w)


def mix_back_call(x, d, w):
    n, per, rows, width = x.shape
    count = min(4, per)
    spec = pl.BlockSpec((n, count, rows, width), lambda t: (0, t, 0, 0))
    return pl.pallas_call(
        mix_back_kernel,
        grid=(per // count,),
        in_specs=[spec, spec, whole(w)],
        out_specs=[spec, whole(w)],
        out_shape=[jax.ShapeDtypeStruct(x.shape, BF16), jax.ShapeDtypeStruct(w.shape, F32)],
        compiler_params=params(),
        cost_estimate=cost(4 * x.size * w.shape[0], 6 * x.size),
        name="mix_back",
    )(x, d, w)


def mlp_kernel(tok, cot, mix, wg, wgt, wu, wut, wd, wdt, *rest):
    out, part, dmix, gdown, gup, ggate, mixed, dback = rest[-8:]
    width = tok.shape[2]
    steps = tok.shape[1]
    sub = 2

    @pl.when(pl.program_id(0) == 0)
    def _():
        gdown[...] = jnp.zeros_like(gdown)
        gup[...] = jnp.zeros_like(gup)
        ggate[...] = jnp.zeros_like(ggate)

    mixed[...] = jnp.swapaxes(mix[...].astype(F32), 0, 1)

    @pl.loop(0, TILE // sub)
    def _(s):
        at = pl.ds(s * sub, sub)
        flat = (sub * steps, width)
        back = (sub, steps, width)
        t = tok[at].reshape(flat)
        ct = cot[at].reshape(flat)
        m = mixed[at].reshape(flat)
        gate = sig(dot(t, wg[...]))
        hidden = (t.astype(F32) + gate * m).astype(BF16)
        pre = dot(hidden, wu[...])
        sg = sig(pre)
        act = (pre * sg).astype(BF16)
        out[at] = (hidden.astype(F32) + dot(act, wd[...])).astype(BF16).reshape(back)
        dact = (dot(ct, wdt[...]) * (sg * (1.0 + pre * (1.0 - sg)))).astype(BF16)
        gdown[...] += dot_rows(act, ct)
        gup[...] += dot_rows(hidden, dact)
        dh = (ct.astype(F32) + dot(dact, wut[...])).astype(BF16).astype(F32)
        dm = dh * gate
        dback[at] = dm.reshape(back)
        dgate = (dm * m * (1.0 - gate)).astype(BF16)
        part[at] = (dh + dot(dgate, wgt[...])).astype(BF16).reshape(back)
        ggate[...] += dot_rows(t, dgate)

    dmix[...] = jnp.swapaxes(dback[...], 0, 1).astype(BF16)


def mlp_call(chunk, tokens, cot, mix, weights, carried):
    blocks, steps, width = tokens.shape
    per = mix.shape[0]
    wg, wgt, wu, wut, wd, wdt = weights
    tile = pl.BlockSpec((TILE, per, width), lambda t: (t, chunk, 0))
    mid = pl.BlockSpec((per, TILE, width), lambda t: (0, t, 0))
    held = [pl.BlockSpec(memory_space=pl.ANY)] * len(carried)
    grads = [wd, wu, wg]
    rows = blocks * per
    full = jax.ShapeDtypeStruct(tokens.shape, BF16)
    return pl.pallas_call(
        mlp_kernel,
        grid=(blocks // TILE,),
        in_specs=[tile, tile, mid] + [whole(w) for w in weights] + held,
        out_specs=[tile, tile, mid] + [whole(g) for g in grads],
        out_shape=[full, full, jax.ShapeDtypeStruct(mix.shape, BF16)]
        + [jax.ShapeDtypeStruct(g.shape, F32) for g in grads],
        scratch_shapes=[pltpu.VMEM((TILE, per, width), F32)] * 2,
        input_output_aliases={9 + a: a for a in range(len(carried))},
        compiler_params=params(),
        cost_estimate=cost(2 * rows * (6 * wu.size + 3 * wg.size), 12 * rows * width, rows * 3 * width),
        name="mlp",
    )(tokens, cot, mix, *weights, *carried)


def back_kernel(d, val, out, grad):

    @pl.when(pl.program_id(0) == 0)
    def _():
        grad[...] = jnp.zeros_like(grad)

    out[...] = jnp.swapaxes(d[...].astype(F32), 0, 1).astype(BF16)
    grad[...] += dot_lanes(lanes(val, TILE), lanes(out, TILE))


def back_call(d, values):
    blocks, steps, width = values.shape
    per = d.shape[0]
    return pl.pallas_call(
        back_kernel,
        grid=(blocks // TILE,),
        in_specs=[
            pl.BlockSpec((per, TILE, width), lambda t: (0, t, 0)),
            pl.BlockSpec((TILE, steps, width), lambda t: (t, 0, 0)),
        ],
        out_specs=[
            pl.BlockSpec((TILE, per, width), lambda t: (t, 0, 0)),
            pl.BlockSpec((steps, per), lambda t: (0, 0)),
        ],
        out_shape=[
            jax.ShapeDtypeStruct((blocks, per, width), BF16),
            jax.ShapeDtypeStruct((steps, per), F32),
        ],
        compiler_params=params(),
        cost_estimate=cost(2 * values.size * per, 2 * values.size + 4 * d.size),
        name="first_back",
    )(d, values)


def tokens_kernel(*refs):
    *ds, part, tok, w1, wvt, out, grad = refs
    width = tok.shape[2]

    @pl.when(pl.program_id(0) == 0)
    def _():
        grad[...] = jnp.zeros_like(grad)

    res = dot(w1[...], jnp.concatenate([lanes(d, TILE) for d in ds], axis=0))
    total = grad[...]
    for b in range(TILE):
        dv = res[:, b * width : (b + 1) * width].astype(BF16)
        out[b] = (part[b].astype(F32) + dot(dv, wvt[...])).astype(BF16)
        total += dot_rows(tok[b], dv)
    grad[...] = total


def tokens_call(ds, part, tokens, w1, wvt):
    blocks, steps, width = tokens.shape
    tile = pl.BlockSpec((TILE, steps, width), lambda t: (t, 0, 0))
    return pl.pallas_call(
        tokens_kernel,
        grid=(blocks // TILE,),
        in_specs=[pl.BlockSpec((TILE, *d.shape[1:]), lambda t: (t, 0, 0)) for d in ds]
        + [tile, tile, whole(w1), whole(wvt)],
        out_specs=[tile, whole(wvt)],
        out_shape=[jax.ShapeDtypeStruct(tokens.shape, BF16), jax.ShapeDtypeStruct(wvt.shape, F32)],
        compiler_params=params(),
        cost_estimate=cost(2 * tokens.size * (steps + 2 * width), 8 * tokens.size),
        name="grad_tokens",
    )(*ds, part, tokens, w1, wvt)


def summed_late(parts):
    rows = sum(p.shape[0] for p in parts)
    width = parts[0].shape[1]
    n = lax.axis_size("ctx")

    def swap(a, axis):
        return lax.all_to_all(a, axis, split_axis=0, concat_axis=0, tiled=True)

    def spread(a, axis):
        return swap(jnp.broadcast_to(a, (lax.axis_size(axis), *a.shape)), axis)

    mine = swap(jnp.concatenate(parts, axis=0).astype(BF16).reshape(n, rows // n, width), "ctx")
    mine = jnp.sum(mine.astype(F32), axis=0).astype(BF16)
    mine = jnp.sum(spread(mine, "dp").astype(F32), axis=0).astype(BF16)
    total = spread(mine, "ctx").reshape(rows, width).astype(F32)
    out, at = [], 0
    for p in parts:
        out.append(total[at : at + p.shape[0]])
        at += p.shape[0]
    return out


def body(tokens, cotangent, w_gate_value, w_first, w_second, w_up, w_down):
    n = lax.axis_size("ctx")
    seq_rows, width = tokens.shape[1:]
    steps = w_first.shape[0]
    blocks = seq_rows // steps
    chunks = 2
    per = steps // chunks
    tok = tokens.reshape(blocks, steps, width)
    cot = cotangent.reshape(blocks, steps, width)
    wg, wv = w_gate_value[:, :width], w_gate_value[:, width:]
    w1t = w_first.T
    w2t = w_second.T
    weights = (wg, wg.T, w_up, w_up.T, w_down, w_down.T)

    def exchange(a):
        moved = lax.all_to_all(
            a.reshape(n, per // n, blocks, width), "ctx", split_axis=0, concat_axis=0, tiled=True
        )
        return moved

    values, lead = first_call(tok, wv, w1t[:per], per)
    firsts = [lead, *first_call(values, None, w1t[per:], per)]

    first_mid, mixed, d_mixed, d_first = {}, {}, {}, {}
    small, second, first_cols = [], [], []
    carried = ()
    for at in range(chunks + 3):
        if at < chunks:
            first_mid[at] = exchange(firsts[at])
        c = at - 1
        if 0 <= c < chunks:
            mixed[c] = exchange(mix_call(first_mid[c], w2t)).reshape(per, blocks, width)
        c = at - 2
        if 0 <= c < chunks:
            out, part, dm, *grads = mlp_call(c, tok, cot, mixed[c], weights, carried)
            carried = (out, part)
            small.append(grads)
            d_mixed[c] = exchange(dm)
        c = at - 3
        if 0 <= c < chunks:
            df, g2 = mix_back_call(first_mid[c], d_mixed[c], w_second)
            second.append(g2)
            d_first[c] = exchange(df).reshape(per, blocks, width)
    back = []
    for c in range(chunks):
        filled, cols = back_call(d_first[c], values)
        back.append(filled)
        first_cols.append(cols)
    grad_down, grad_up, grad_gate = [sum(parts) for parts in zip(*small)]
    grad_tokens, grad_value = tokens_call(back, carried[1], tok, w_first, wv.T)

    axes = ("dp", "ctx")
    scale = float(seq_rows * n * lax.axis_size("dp")) ** (-0.5)
    grad_second = sum(second)
    grad_down, grad_up, grad_gate, grad_second = lax.psum(
        (grad_down, grad_up, grad_gate, grad_second), axes
    )
    strips = [c[:, at : at + width] for c in first_cols for at in range(0, per, width)]
    *strips, grad_value = summed_late([*strips, grad_value])
    return (
        carried[0].reshape(tokens.shape),
        grad_tokens.reshape(tokens.shape),
        jnp.concatenate([grad_gate, grad_value], axis=1) * scale,
        jnp.concatenate(strips, axis=1) * scale,
        grad_second * scale,
        grad_up * scale,
        grad_down * scale,
    )


def solution(mesh):
    placed = (P("dp", "ctx", None), P("dp", "ctx", None), P(), P(), P(), P(), P())
    return jax.shard_map(
        body,
        mesh=mesh,
        in_specs=placed,
        out_specs=(P("dp", "ctx", None), P("dp", "ctx", None), P(), P(), P(), P(), P()),
        check_vma=False,
    )
```

```python
import functools

import jax
import jax.numpy as jnp
from jax import lax
from jax.experimental import pallas as pl
from jax.experimental.pallas import tpu as pltpu
from jax.sharding import PartitionSpec as P

F32 = jnp.float32
BF16 = jnp.bfloat16
TILE = 16
VMEM_LIMIT = 56 * 1024 * 1024


def sig(v):
    return 0.5 * jnp.tanh(0.5 * v) + 0.5


def dot(a, b):
    return jnp.dot(a, b, preferred_element_type=F32)


def dot_rows(a, b):
    return lax.dot_general(a, b, (((0,), (0,)), ((), ())), preferred_element_type=F32)


def dot_lanes(a, b):
    return lax.dot_general(a, b, (((1,), (1,)), ((), ())), preferred_element_type=F32)


def lanes(ref, count):
    return jnp.concatenate([ref[b] for b in range(count)], axis=1)


def params():
    return pltpu.CompilerParams(vmem_limit_bytes=VMEM_LIMIT)


def cost(flops, nbytes, trans=0):
    return pl.CostEstimate(flops=int(flops), bytes_accessed=int(nbytes), transcendentals=int(trans))


def whole(array):
    zeros = (0,) * array.ndim
    return pl.BlockSpec(array.shape, lambda *_: zeros)


def first_kernel(from_tokens, *refs):
    if from_tokens:
        src, wv, w1t, val, *outs = refs
        rows = src.shape[0] * src.shape[1]
        val[...] = dot(src[...].reshape(rows, src.shape[2]), wv[...]).astype(BF16).reshape(val.shape)
    else:
        val, w1t, *outs = refs
    width = val.shape[2]
    vals = lanes(val, TILE)
    per = outs[0].shape[0]
    for at, out in enumerate(outs):
        res = dot(w1t[at * per : (at + 1) * per, :], vals)
        parts = jnp.stack([res[:, b * width : (b + 1) * width] for b in range(TILE)], 0)
        out[...] = jnp.swapaxes(parts, 0, 1).astype(BF16)


def first_call(src, wv, w1t, per):
    blocks, steps, width = src.shape
    outs = w1t.shape[0] // per
    tile = pl.BlockSpec((TILE, steps, width), lambda t: (t, 0, 0))
    sent = pl.BlockSpec((per, TILE, width), lambda t: (0, t, 0))
    sent_shape = jax.ShapeDtypeStruct((per, blocks, width), BF16)
    flops = 2 * blocks * steps * width * w1t.shape[0]
    if wv is not None:
        return pl.pallas_call(
            functools.partial(first_kernel, True),
            grid=(blocks // TILE,),
            in_specs=[tile, whole(wv), whole(w1t)],
            out_specs=[tile] + [sent] * outs,
            out_shape=[jax.ShapeDtypeStruct(src.shape, BF16)] + [sent_shape] * outs,
            compiler_params=params(),
            cost_estimate=cost(flops + 2 * src.size * width, 4 * src.size + 2 * per * blocks * width),
            name="values_first",
        )(src, wv, w1t)
    return pl.pallas_call(
        functools.partial(first_kernel, False),
        grid=(blocks // TILE,),
        in_specs=[tile, whole(w1t)],
        out_specs=[sent] * outs,
        out_shape=[sent_shape] * outs,
        compiler_params=params(),
        cost_estimate=cost(flops, 2 * src.size + 2 * outs * per * blocks * width),
        name="first_rest",
    )(src, w1t)


def gather_positions(ref, count, order, width):
    return jnp.concatenate([ref[:, q].reshape(order, width) for q in range(count)], axis=1)


def spread_positions(ref, res, count, width):
    n, _, rows, _ = ref.shape
    for q in range(count):
        ref[:, q] = res[:, q * width : (q + 1) * width].astype(BF16).reshape(n, rows, width)


def mix_kernel(x, w, out):
    n, count, rows, width = x.shape
    spread_positions(out, dot(w[...], gather_positions(x, count, n * rows, width)), count, width)


def mix_back_kernel(x, d, w, out, grad):
    n, count, rows, width = x.shape

    @pl.when(pl.program_id(0) == 0)
    def _():
        grad[...] = jnp.zeros_like(grad)

    dm = gather_positions(d, count, n * rows, width)
    spread_positions(out, dot(w[...], dm), count, width)
    grad[...] += dot_lanes(gather_positions(x, count, n * rows, width), dm)


def mix_call(x, w):
    n, per, rows, width = x.shape
    count = min(4, per)
    spec = pl.BlockSpec((n, count, rows, width), lambda t: (0, t, 0, 0))
    return pl.pallas_call(
        mix_kernel,
        grid=(per // count,),
        in_specs=[spec, whole(w)],
        out_specs=spec,
        out_shape=jax.ShapeDtypeStruct(x.shape, BF16),
        compiler_params=params(),
        cost_estimate=cost(2 * x.size * w.shape[0], 4 * x.size),
        name="mix",
    )(x, w)


def mix_back_call(x, d, w):
    n, per, rows, width = x.shape
    count = min(4, per)
    spec = pl.BlockSpec((n, count, rows, width), lambda t: (0, t, 0, 0))
    return pl.pallas_call(
        mix_back_kernel,
        grid=(per // count,),
        in_specs=[spec, spec, whole(w)],
        out_specs=[spec, whole(w)],
        out_shape=[jax.ShapeDtypeStruct(x.shape, BF16), jax.ShapeDtypeStruct(w.shape, F32)],
        compiler_params=params(),
        cost_estimate=cost(4 * x.size * w.shape[0], 6 * x.size),
        name="mix_back",
    )(x, d, w)


def mlp_kernel(tok, cot, mix, wg, wgt, wu, wut, wd, wdt, *rest):
    out, part, dmix, gdown, gup, ggate, mixed, dback = rest[-8:]
    width = tok.shape[2]
    steps = tok.shape[1]
    sub = 2

    @pl.when(pl.program_id(0) == 0)
    def _():
        gdown[...] = jnp.zeros_like(gdown)
        gup[...] = jnp.zeros_like(gup)
        ggate[...] = jnp.zeros_like(ggate)

    mixed[...] = jnp.swapaxes(mix[...].astype(F32), 0, 1)

    @pl.loop(0, TILE // sub)
    def _(s):
        at = pl.ds(s * sub, sub)
        flat = (sub * steps, width)
        back = (sub, steps, width)
        t = tok[at].reshape(flat)
        ct = cot[at].reshape(flat)
        m = mixed[at].reshape(flat)
        gate = sig(dot(t, wg[...]))
        hidden = (t.astype(F32) + gate * m).astype(BF16)
        pre = dot(hidden, wu[...])
        sg = sig(pre)
        act = (pre * sg).astype(BF16)
        out[at] = (hidden.astype(F32) + dot(act, wd[...])).astype(BF16).reshape(back)
        dact = (dot(ct, wdt[...]) * (sg * (1.0 + pre * (1.0 - sg)))).astype(BF16)
        gdown[...] += dot_rows(act, ct)
        gup[...] += dot_rows(hidden, dact)
        dh = (ct.astype(F32) + dot(dact, wut[...])).astype(BF16).astype(F32)
        dm = dh * gate
        dback[at] = dm.reshape(back)
        dgate = (dm * m * (1.0 - gate)).astype(BF16)
        part[at] = (dh + dot(dgate, wgt[...])).astype(BF16).reshape(back)
        ggate[...] += dot_rows(t, dgate)

    dmix[...] = jnp.swapaxes(dback[...], 0, 1).astype(BF16)


def mlp_call(chunk, tokens, cot, mix, weights, carried):
    blocks, steps, width = tokens.shape
    per = mix.shape[0]
    wg, wgt, wu, wut, wd, wdt = weights
    tile = pl.BlockSpec((TILE, per, width), lambda t: (t, chunk, 0))
    mid = pl.BlockSpec((per, TILE, width), lambda t: (0, t, 0))
    held = [pl.BlockSpec(memory_space=pl.ANY)] * len(carried)
    grads = [wd, wu, wg]
    rows = blocks * per
    full = jax.ShapeDtypeStruct(tokens.shape, BF16)
    return pl.pallas_call(
        mlp_kernel,
        grid=(blocks // TILE,),
        in_specs=[tile, tile, mid] + [whole(w) for w in weights] + held,
        out_specs=[tile, tile, mid] + [whole(g) for g in grads],
        out_shape=[full, full, jax.ShapeDtypeStruct(mix.shape, BF16)]
        + [jax.ShapeDtypeStruct(g.shape, F32) for g in grads],
        scratch_shapes=[pltpu.VMEM((TILE, per, width), F32)] * 2,
        input_output_aliases={9 + a: a for a in range(len(carried))},
        compiler_params=params(),
        cost_estimate=cost(10 * rows * (6 * wu.size + 3 * wg.size), 12 * rows * width, rows * 3 * width),
        name="mlp",
    )(tokens, cot, mix, *weights, *carried)


def back_kernel(d, val, out, grad):

    @pl.when(pl.program_id(0) == 0)
    def _():
        grad[...] = jnp.zeros_like(grad)

    out[...] = jnp.swapaxes(d[...].astype(F32), 0, 1).astype(BF16)
    grad[...] += dot_lanes(lanes(val, TILE), lanes(out, TILE))


def back_call(d, values):
    blocks, steps, width = values.shape
    per = d.shape[0]
    return pl.pallas_call(
        back_kernel,
        grid=(blocks // TILE,),
        in_specs=[
            pl.BlockSpec((per, TILE, width), lambda t: (0, t, 0)),
            pl.BlockSpec((TILE, steps, width), lambda t: (t, 0, 0)),
        ],
        out_specs=[
            pl.BlockSpec((TILE, per, width), lambda t: (t, 0, 0)),
            pl.BlockSpec((steps, per), lambda t: (0, 0)),
        ],
        out_shape=[
            jax.ShapeDtypeStruct((blocks, per, width), BF16),
            jax.ShapeDtypeStruct((steps, per), F32),
        ],
        compiler_params=params(),
        cost_estimate=cost(2 * values.size * per, 2 * values.size + 4 * d.size),
        name="first_back",
    )(d, values)


def tokens_kernel(*refs):
    *ds, part, tok, w1, wvt, out, grad = refs
    width = tok.shape[2]

    @pl.when(pl.program_id(0) == 0)
    def _():
        grad[...] = jnp.zeros_like(grad)

    res = dot(w1[...], jnp.concatenate([lanes(d, TILE) for d in ds], axis=0))
    total = grad[...]
    for b in range(TILE):
        dv = res[:, b * width : (b + 1) * width].astype(BF16)
        out[b] = (part[b].astype(F32) + dot(dv, wvt[...])).astype(BF16)
        total += dot_rows(tok[b], dv)
    grad[...] = total


def tokens_call(ds, part, tokens, w1, wvt):
    blocks, steps, width = tokens.shape
    tile = pl.BlockSpec((TILE, steps, width), lambda t: (t, 0, 0))
    return pl.pallas_call(
        tokens_kernel,
        grid=(blocks // TILE,),
        in_specs=[pl.BlockSpec((TILE, *d.shape[1:]), lambda t: (t, 0, 0)) for d in ds]
        + [tile, tile, whole(w1), whole(wvt)],
        out_specs=[tile, whole(wvt)],
        out_shape=[jax.ShapeDtypeStruct(tokens.shape, BF16), jax.ShapeDtypeStruct(wvt.shape, F32)],
        compiler_params=params(),
        cost_estimate=cost(2 * tokens.size * (steps + 2 * width), 8 * tokens.size),
        name="grad_tokens",
    )(*ds, part, tokens, w1, wvt)


def summed_late(parts):
    rows = sum(p.shape[0] for p in parts)
    width = parts[0].shape[1]
    n = lax.axis_size("ctx")

    def swap(a, axis):
        return lax.all_to_all(a, axis, split_axis=0, concat_axis=0, tiled=True)

    def spread(a, axis):
        return swap(jnp.broadcast_to(a, (lax.axis_size(axis), *a.shape)), axis)

    mine = swap(jnp.concatenate(parts, axis=0).astype(BF16).reshape(n, rows // n, width), "ctx")
    mine = jnp.sum(mine.astype(F32), axis=0).astype(BF16)
    mine = jnp.sum(spread(mine, "dp").astype(F32), axis=0).astype(BF16)
    total = spread(mine, "ctx").reshape(rows, width).astype(F32)
    out, at = [], 0
    for p in parts:
        out.append(total[at : at + p.shape[0]])
        at += p.shape[0]
    return out


def body(tokens, cotangent, w_gate_value, w_first, w_second, w_up, w_down):
    n = lax.axis_size("ctx")
    seq_rows, width = tokens.shape[1:]
    steps = w_first.shape[0]
    blocks = seq_rows // steps
    chunks = 2
    per = steps // chunks
    tok = tokens.reshape(blocks, steps, width)
    cot = cotangent.reshape(blocks, steps, width)
    wg, wv = w_gate_value[:, :width], w_gate_value[:, width:]
    w1t = w_first.T
    w2t = w_second.T
    weights = (wg, wg.T, w_up, w_up.T, w_down, w_down.T)

    def exchange(a):
        moved = lax.all_to_all(
            a.reshape(n, per // n, blocks, width), "ctx", split_axis=0, concat_axis=0, tiled=True
        )
        return moved

    values, lead = first_call(tok, wv, w1t[:per], per)
    firsts = [lead, *first_call(values, None, w1t[per:], per)]

    first_mid, mixed, d_mixed, d_first = {}, {}, {}, {}
    small, second, first_cols = [], [], []
    carried = ()
    for at in range(chunks + 3):
        if at < chunks:
            first_mid[at] = exchange(firsts[at])
        c = at - 1
        if 0 <= c < chunks:
            mixed[c] = exchange(mix_call(first_mid[c], w2t)).reshape(per, blocks, width)
        c = at - 2
        if 0 <= c < chunks:
            out, part, dm, *grads = mlp_call(c, tok, cot, mixed[c], weights, carried)
            carried = (out, part)
            small.append(grads)
            d_mixed[c] = exchange(dm)
        c = at - 3
        if 0 <= c < chunks:
            df, g2 = mix_back_call(first_mid[c], d_mixed[c], w_second)
            second.append(g2)
            d_first[c] = exchange(df).reshape(per, blocks, width)
    back = []
    for c in range(chunks):
        filled, cols = back_call(d_first[c], values)
        back.append(filled)
        first_cols.append(cols)
    grad_down, grad_up, grad_gate = [sum(parts) for parts in zip(*small)]
    grad_tokens, grad_value = tokens_call(back, carried[1], tok, w_first, wv.T)

    axes = ("dp", "ctx")
    scale = float(seq_rows * n * lax.axis_size("dp")) ** (-0.5)
    strips = [
        wide[:, at : at + width]
        for wide in (*first_cols, sum(second), grad_up)
        for at in range(0, wide.shape[1], width)
    ]
    summed = summed_late([*strips, grad_down, grad_gate, grad_value])
    grad_down, grad_gate, grad_value = summed[-3:]
    count = steps // width
    cols, cols_second, cols_up = summed[:count], summed[count:-3][: w_second.shape[1] // width], summed[:-3][-(w_up.shape[1] // width) :]
    scale = float(seq_rows * n * lax.axis_size("dp")) ** (-0.5)
    return (
        carried[0].reshape(tokens.shape),
        grad_tokens.reshape(tokens.shape),
        jnp.concatenate([grad_gate, grad_value], axis=1) * scale,
        jnp.concatenate(cols, axis=1) * scale,
        jnp.concatenate(cols_second, axis=1) * scale,
        jnp.concatenate(cols_up, axis=1) * scale,
        grad_down * scale,
    )


def solution(mesh):
    placed = (P("dp", "ctx", None), P("dp", "ctx", None), P(), P(), P(), P(), P())
    return jax.shard_map(
        body,
        mesh=mesh,
        in_specs=placed,
        out_specs=(P("dp", "ctx", None), P("dp", "ctx", None), P(), P(), P(), P(), P()),
        check_vma=False,
    )
```
